32 devices in a mesh: gx: 8 (over z, y), gy: 4 (over x, core).
Axes of the slice: x: 2, y: 2, z: 4, core: 2. Of those that a mesh axis runs over, the one named last changes fastest.
Arguments:
- state: float32 [5, 120, 16384], P(None, None, ('gx', 'gy')), may hold values from -6 to 6
- coef: float32 [5, 5, 16384], P(None, None, ('gx', 'gy')), may hold values from -3 to 3
- basis_quad: float32 [216, 120], replicated, may hold values from -0.5 to 0.5
- test_deriv: float32 [120, 216], replicated, may hold values from -0.3125 to 0.3125
- trace_vec: float32 [120], replicated, may hold values from -0.5 to 0.5
- lift_vec: float32 [120], replicated, may hold values from -3 to 3
- tent_height: float32 [3, 2048], P(None, ('gx', 'gy')), may hold values from 0.2 to 0.4
- elem_tent: int32 [3, 16384], P(None, ('gx', 'gy')), may hold values from 0 to 2047, as said below
Outputs:
- final_state: float32 [5, 120, 16384], P(None, None, ('gx', 'gy'))
The draws below stay inside these ranges and needn't reach their ends.
Inputs may be any that keep to these rules, and one draw needn't show every extreme that they name: `elem_tent`: tent t is owned by device t // 64 of the devices numbered with gx slowest. At every level the owner of an element's tent is the element's own device or one of its four neighbours along gx or gy, with wrap-around. At a level no device hands more than 64 of its elements to one neighbour; in every level some device hands exactly 64 to a neighbour, and some device receives exactly 64 from each of its four neighbours.
All inputs are finite; a program needn't handle non-finite values.
Results may differ from the reference program's by a relative error of at most 0.00011.
Values sent between devices are 32-bit elements; how exact they have to be, the bound alone decides.
A program may use at most 128 MiB of HBM per device.

```python
import jax
import jax.numpy as jnp
from jax import lax

NF = 5
NB = 120
NQ = 216
E_DEV = 512
LEVELS = 3
CAP = 64
TENT_DEV = 64
ELEMS = 16384
TENTS = 2048
N_GX = 8
N_GY = 4


def draw_elem_tent(key, part):
    devices_all = N_GX * N_GY
    rows_all = []
    step_first = jnp.array([1, -1, 0, 0, 0], dtype=jnp.int32)
    step_second = jnp.array([0, 0, 1, -1, 0], dtype=jnp.int32)
    for level_index in range(LEVELS):
        level_key = jax.random.fold_in(key, 7919 + level_index)
        key_counts, key_target, key_order, key_local = jax.random.split(level_key, 4)
        handed = jax.random.randint(key_counts, (devices_all, 4), CAP // 2, CAP + 1)
        target = jax.random.randint(key_target, (), 0, devices_all)
        target_first = target // N_GY
        target_second = target % N_GY
        senders = jnp.stack([(target_first - 1) % N_GX * N_GY + target_second, (target_first + 1) % N_GX * N_GY + target_second, target_first * N_GY + (target_second - 1) % N_GY, target_first * N_GY + (target_second + 1) % N_GY])
        handed = handed.at[senders, jnp.arange(4)].set(CAP)
        ranks = jax.vmap(lambda single: jax.random.permutation(single, E_DEV))(jax.random.split(key_order, devices_all))
        bounds = jnp.cumsum(handed, axis=1)
        heading = jnp.sum((ranks[:, :, None] >= bounds[:, None, :]).astype(jnp.int32), axis=2)
        device_ids = jnp.arange(devices_all, dtype=jnp.int32)
        place_first = device_ids // N_GY
        place_second = device_ids % N_GY
        owner_first = (place_first[:, None] + step_first[heading]) % N_GX
        owner_second = (place_second[:, None] + step_second[heading]) % N_GY
        owner = owner_first * N_GY + owner_second
        local_tent = jax.random.randint(key_local, (devices_all, E_DEV), 0, TENT_DEV)
        rows_all.append((owner * TENT_DEV + local_tent).reshape(-1))
    return jnp.stack(rows_all).astype(jnp.int32)


def block_levels(rng, dims, cuts, least, high):
    def one(dim, shards_of):
        steps = jax.random.uniform(jax.random.fold_in(jax.random.fold_in(rng, 6), dim), (shards_of,), jnp.float32, least / len(cuts), high / len(cuts))
        return jnp.repeat(jnp.exp(steps), dims[dim] // shards_of).reshape((-1,) + (1,) * (len(dims) - dim - 1))

    level = one(*cuts[0])
    for cut in cuts[1:]:
        level = level * one(*cut)
    return level


def scatter_about(rng, dims, deviation, most, cuts=(), kind=jnp.bfloat16):
    values = jax.random.normal(rng, dims, jnp.float32) * deviation
    if len(cuts) > 0:
        values = block_levels(rng, dims, cuts, -0.22, 0.18) * values
    return jnp.clip(values, min=-most, max=most).astype(kind)


def setup_inputs(seed: int = 0) -> dict:
    keys = jax.random.split(jax.random.key(seed), 9)
    state = scatter_about(keys[0], (NF, NB, ELEMS), 1.0, 6.0, ((2, 32),), jnp.float32)
    coef = scatter_about(keys[1], (NF, NF, ELEMS), 0.45, 3.0, ((2, 32),), jnp.float32)
    basis_quad = scatter_about(keys[2], (NQ, NB), NB ** -0.5, 0.5, (), jnp.float32)
    test_deriv = scatter_about(keys[3], (NB, NQ), (2 * NQ) ** -0.5, 0.3125, (), jnp.float32)
    trace_vec = scatter_about(keys[4], (NB,), NB ** -0.5, 0.5, (), jnp.float32)
    lift_vec = scatter_about(keys[5], (NB,), 0.5, 3.0, (), jnp.float32)
    tent_height = jnp.clip(0.2 + 0.2 * jax.random.uniform(keys[6], (LEVELS, TENTS), jnp.float32) ** block_levels(keys[6], (LEVELS, TENTS), ((1, 32),), -0.2, 0.2), 0.2, 0.4)
    elem_tent = draw_elem_tent(jax.random.fold_in(keys[8], 71), 0)
    return {"state": state, "coef": coef, "basis_quad": basis_quad, "test_deriv": test_deriv, "trace_vec": trace_vec, "lift_vec": lift_vec, "tent_height": tent_height, "elem_tent": elem_tent}


def reference(state, coef, basis_quad, test_deriv, trace_vec, lift_vec, tent_height, elem_tent):
    highest = lax.Precision.HIGHEST
    values = state
    for level_index in range(LEVELS):
        tents = elem_tent[level_index]
        counts = jax.ops.segment_sum(jnp.ones(tents.shape, jnp.float32), tents, TENTS)
        safe_counts = jnp.maximum(counts, 1.0)
        heights = tent_height[level_index][tents][None, None, :]

        def derivative(current):
            traces = jnp.einsum("b,fbs->fs", trace_vec, current, precision=highest)
            sums = jax.ops.segment_sum(traces.T, tents, TENTS)
            means = (sums / safe_counts[:, None])[tents].T
            at_points = jnp.einsum("qb,fbs->fqs", basis_quad, current, precision=highest)
            flux_all = jnp.einsum("gfs,fqs->gqs", coef, at_points, precision=highest)
            weak_form = jnp.einsum("bq,gqs->gbs", test_deriv, flux_all, precision=highest)
            return weak_form + lift_vec[None, :, None] * (means - traces)[:, None, :]

        first = derivative(values)
        second = derivative(first)
        third = derivative(second)
        values = values + heights * first + heights * heights / 2.0 * second + heights * heights * heights / 6.0 * third
    return values
```

```python
import functools

import jax
import jax.numpy as jnp
from jax import lax
from jax.experimental import pallas as pl
from jax.experimental.pallas import tpu as pltpu
from jax.sharding import PartitionSpec as P

F32 = jnp.float32
BF16 = jnp.bfloat16
HIGHEST = lax.Precision.HIGHEST
MESH = pl.DeviceIdType.MESH
SCALE = 8.0
ROWS = 16
LANES = 128


def up(n, m):
    return -(-n // m) * m


def dot32(a, b):
    return jnp.dot(a, b, precision=HIGHEST, preferred_element_type=F32)


def split2(x):
    hi = x.astype(BF16)
    lo = (x - hi.astype(F32)).astype(BF16)
    return hi, lo


def split3(x):
    hi = x.astype(BF16)
    rest = x - hi.astype(F32)
    mid = rest.astype(BF16)
    lo = (rest - mid.astype(F32)).astype(BF16)
    return jnp.concatenate([hi, mid, lo], axis=0)


def fold3(x):
    n = x.shape[0] // 3
    return x[:n] + (x[n : 2 * n] + x[2 * n :])


def seg_sum(x, onehot):
    return fold3(
        lax.dot_general(
            split3(x), onehot, (((1,), (1,)), ((), ())), preferred_element_type=F32
        )
    )


def seg_take(x, onehot):
    return fold3(jnp.dot(split3(x), onehot, preferred_element_type=F32))


def kernel(
    sizes,
    state_ref,
    coef_ref,
    bq_ref,
    td_ref,
    trace_ref,
    lift_ref,
    height_ref,
    tent_ref,
    out_ref,
    hot_ref,
    lhs_ref,
    cs_ref,
    mom_ref,
    x_ref,
    d_ref,
    cur_ref,
    g_ref,
    stat_ref,
    stat_in,
    part_ref,
    part_in,
    tot_ref,
    tot_in,
    send_sem,
    recv_sem,
):
    n_first, n_second = sizes
    fields, basis, n_elem = state_ref.shape
    levels, tent_dev = height_ref.shape
    pair = 2 * tent_dev
    wide = up(basis, LANES)
    crows = cs_ref.shape[0]
    me_first = lax.axis_index("gx")
    me_second = lax.axis_index("gy")
    next_first = lax.rem(me_first + 1, n_first)
    prev_first = lax.rem(me_first + n_first - 1, n_first)
    next_second = lax.rem(me_second + 1, n_second)
    prev_second = lax.rem(me_second + n_second - 1, n_second)
    peers = [
        (next_first, me_second),
        (prev_first, me_second),
        (me_first, next_second),
        (me_first, prev_second),
    ]

    barrier = pltpu.get_barrier_semaphore()
    for peer in peers:
        pl.semaphore_signal(barrier, inc=1, device_id=peer, device_id_type=MESH)

    def remote(src, dst, slot, k):
        return pltpu.make_async_remote_copy(
            src_ref=src,
            dst_ref=dst,
            send_sem=send_sem.at[slot, k],
            recv_sem=recv_sem.at[slot, k],
            device_id=peers[k],
            device_id_type=MESH,
        )

    cs_ref[...] = jnp.zeros_like(cs_ref)
    for g in range(fields):
        cs_ref[g * fields : (g + 1) * fields, :] = coef_ref[g]
    cs_ref[fields * fields : fields * fields + 1, :] = jnp.ones((1, n_elem), F32)
    for level in range(levels):
        tents = tent_ref[level : level + 1, :]
        owner = tents // tent_dev
        local = tents - owner * tent_dev
        own_first = owner // n_second
        own_second = owner - own_first * n_second
        base = jnp.where(
            own_first == me_first,
            jnp.where(
                own_second == me_second,
                0,
                jnp.where(own_second == next_second, 2 * pair, 2 * pair + tent_dev),
            ),
            jnp.where(own_first == next_first, pair, pair + tent_dev),
        )
        column = base + local
        rows = lax.broadcasted_iota(jnp.int32, (3 * pair, n_elem), 0)
        hot_ref[level] = jnp.where(rows == column, 1.0, 0.0).astype(F32).astype(BF16)

    stat_ref[...] = jnp.zeros_like(stat_ref)
    for level in range(levels):
        sums = seg_sum(cs_ref[...], hot_ref[level])
        for block in range(3):
            stat_ref[block, level * crows : (level + 1) * crows, :] = sums[
                :, block * pair : (block + 1) * pair
            ]
    hrow = levels * crows
    for block in range(3):
        stat_ref[block, hrow : hrow + levels, 0:tent_dev] = SCALE * height_ref[...]
    pl.semaphore_wait(barrier, 4)
    stat_copies = [
        remote(stat_ref.at[1 + k // 2], stat_in.at[k], 0, k) for k in range(4)
    ]
    for copy in stat_copies:
        copy.start()

    a = dot32(td_ref[...] * (1.0 / SCALE), bq_ref[...])
    a2 = dot32(a, a)
    a4 = dot32(a2, a2)
    lift_row = lift_ref[...] * (1.0 / SCALE)
    r0 = trace_ref[...]
    r1 = dot32(r0, a)
    r01 = jnp.concatenate([r0, r1], axis=0)
    r23 = dot32(r01, a2)
    r03 = jnp.concatenate([r01, r23], axis=0)
    r47 = dot32(r03, a4)
    r8 = dot32(r47[3:4], a)
    powers = jnp.concatenate(
        [r03, r47, r8, jnp.zeros((ROWS - 9, basis), F32)], axis=0
    )
    tau = jnp.sum(powers * lift_row, axis=1, keepdims=True)
    tau1 = tau[1:2]

    p_hi, p_lo = split2(powers)
    p_all = jnp.concatenate([p_hi, p_lo], axis=0)
    for f in range(fields):
        s_hi, s_lo = split2(state_ref[f])
        both = jnp.dot(p_all, s_hi, preferred_element_type=F32)
        rest = jnp.dot(p_hi, s_lo, preferred_element_type=F32)
        mom_ref[f] = both[:ROWS] + (both[ROWS:] + rest)

    eye = lax.broadcasted_iota(jnp.int32, (basis, basis), 0) == (
        lax.broadcasted_iota(jnp.int32, (basis, basis), 1)
    )
    lift_col = jnp.sum(jnp.where(eye, lift_row, 0.0), axis=1, keepdims=True)
    cur_ref[...] = jnp.zeros_like(cur_ref)
    cur_ref[0, :, 0:basis] = a
    cur_ref[0, :, basis : basis + 1] = lift_col
    a_hi, a_lo = split2(
        jnp.concatenate(
            [cur_ref[0, :, 0:wide], jnp.zeros((wide - basis, wide), F32)], axis=0
        )
    )
    lhs_ref[...] = jnp.concatenate(
        [
            jnp.concatenate([a_hi, a_hi], axis=1),
            jnp.concatenate([a_lo, a_lo], axis=1),
        ],
        axis=0,
    )

    def coef_row(g, f):
        return coef_ref[g, f : f + 1, :]

    def mix(values):
        result = []
        for g in range(fields):
            total = coef_row(g, 0) * values[0]
            for f in range(1, fields):
                total = total + coef_row(g, f) * values[f]
            result.append(total)
        return result

    def shift(values):
        return [pltpu.roll(v, ROWS - 1, 0) for v in values]

    chunk = g_ref.shape[2]

    def advance(level, part):
        lo_lane = part * chunk
        lanes = slice(lo_lane, lo_lane + chunk)
        source = state_ref if level == 0 else out_ref
        h = d_ref[level, 3 * fields : 3 * fields + 1, lanes]
        weights = [h, h * h * 0.5, h * h * h * (1.0 / 6.0)]
        for section in range(3):
            for tile in range(chunk // LANES):
                at = slice(lo_lane + tile * LANES, lo_lane + (tile + 1) * LANES)
                here = slice(tile * LANES, (tile + 1) * LANES)
                bc = [
                    [
                        jnp.broadcast_to(coef_ref[g, f : f + 1, at], (16, LANES))
                        for f in range(fields)
                    ]
                    for g in range(fields)
                ]
                first = lax.broadcasted_iota(jnp.int32, (wide - basis, LANES), 0) == 0
                for row in range(0, wide, 16):
                    size = min(16, basis - row)
                    if section == 0:
                        v = [source[f, row : row + size, at] for f in range(fields)]
                    else:
                        v = [cur_ref[f, row : row + size, here] for f in range(fields)]
                    for g in range(fields):
                        total = bc[g][0][:size] * v[0]
                        for f in range(1, fields):
                            total = total + bc[g][f][:size] * v[f]
                        if size < 16:
                            drow = section * fields + g
                            tail = jnp.where(
                                first, d_ref[level, drow : drow + 1, at], 0.0
                            )
                            total = jnp.concatenate([total, tail], axis=0)
                        hi, lo = split2(total)
                        g_ref[g, row : row + 16, here] = hi
                        g_ref[g, wide + row : wide + row + 16, here] = lo
            for g in range(fields):
                res = jnp.dot(lhs_ref[...], g_ref[g], preferred_element_type=F32)
                deriv = res[:basis] + res[wide : wide + basis]
                if section < 2:
                    cur_ref[g] = deriv
                prior = source[g, :, lanes] if section == 0 else out_ref[g, :, lanes]
                out_ref[g, :, lanes] = prior + weights[section] * deriv

    lane = lax.broadcasted_iota(jnp.int32, (ROWS, pair), 1)
    copies = list(stat_copies)
    parts = n_elem // chunk
    for level in range(levels):
        moments = [mom_ref[f] for f in range(fields)]
        lead = mix(shift(moments))
        for f in range(fields):
            x_ref[f : f + 1, :] = moments[f][0:1]
            x_ref[fields + f : fields + f + 1, :] = lead[f][0:1]
        inner = [lead[f][1:2] - tau1 * moments[f][0:1] for f in range(fields)]
        for g, value in enumerate(mix(inner)):
            x_ref[2 * fields + g : 2 * fields + g + 1, :] = value
        x_ref[3 * fields : ROWS, :] = jnp.zeros((ROWS - 3 * fields, n_elem), F32)
        sums = seg_sum(x_ref[...], hot_ref[level])
        for block in range(2):
            part_ref[level, block] = sums[:, (1 + block) * pair : (2 + block) * pair]
        going = [
            remote(part_ref.at[level, k // 2], part_in.at[level, k], 1 + level, k)
            for k in range(4)
        ]
        for copy in going:
            copy.start()
        if level > 0:
            for part in range(parts // 2):
                advance(level - 1, part)
        if level == 0:
            for copy in stat_copies:
                copy.wait_recv()
        for copy in going:
            copy.wait_recv()
        own = sums[:, :pair]
        own = own + part_in[level, 0] + part_in[level, 2]
        own = own + pltpu.roll(part_in[level, 1] + part_in[level, 3], tent_dev, 1)
        srows = slice(level * crows, (level + 1) * crows)
        stat = stat_ref[0, srows] + stat_in[0, srows] + stat_in[2, srows]
        stat = stat + pltpu.roll(stat_in[1, srows] + stat_in[3, srows], tent_dev, 1)
        count = jnp.maximum(stat[fields * fields : fields * fields + 1], 1.0)
        mean0 = [own[f : f + 1] / count for f in range(fields)]
        for f in range(fields):
            tot_ref[level, f : f + 1, :] = mean0[f]
            tot_ref[level, fields + f : fields + f + 1, :] = (
                own[fields + f : fields + f + 1] / count
            )
            joint = stat[f * fields : f * fields + 1] * mean0[0]
            for s in range(1, fields):
                joint = joint + stat[f * fields + s : f * fields + s + 1] * mean0[s]
            row = 2 * fields + f
            tot_ref[level, row : row + 1, :] = (
                own[row : row + 1] + tau1 * joint
            ) / count
        tot_ref[level, 3 * fields : ROWS, :] = jnp.broadcast_to(
            stat_ref[0, hrow + level : hrow + level + 1], (ROWS - 3 * fields, pair)
        )
        back = [
            remote(tot_ref.at[level], tot_in.at[level, k], 1 + levels + level, k)
            for k in range(4)
        ]
        for copy in back:
            copy.start()
        copies += going + back
        if level > 0:
            for part in range(parts // 2, parts):
                advance(level - 1, part)
        for copy in back:
            copy.wait_recv()
        low = lane < tent_dev
        table = jnp.concatenate(
            [
                tot_ref[level],
                jnp.where(low, tot_in[level, 1], pltpu.roll(tot_in[level, 0], tent_dev, 1)),
                jnp.where(low, tot_in[level, 3], pltpu.roll(tot_in[level, 2], tent_dev, 1)),
            ],
            axis=1,
        )
        each = seg_take(table, hot_ref[level])
        h = each[3 * fields : 3 * fields + 1]
        d_ref[level, 3 * fields : ROWS, :] = each[3 * fields : ROWS]
        d0 = [each[f : f + 1] - moments[f][0:1] for f in range(fields)]
        n1 = [lead[f] + tau * d0[f] for f in range(fields)]
        d1 = [each[fields + f : fields + f + 1] - n1[f][0:1] for f in range(fields)]
        n2 = mix(shift(n1))
        n2 = [n2[f] + tau * d1[f] for f in range(fields)]
        d2 = [
            each[2 * fields + f : 2 * fields + f + 1] - n2[f][0:1]
            for f in range(fields)
        ]
        for f in range(fields):
            d_ref[level, f : f + 1, :] = d0[f]
            d_ref[level, fields + f : fields + f + 1, :] = d1[f]
            d_ref[level, 2 * fields + f : 2 * fields + f + 1, :] = d2[f]
        if level < levels - 1:
            n3 = mix(shift(n2))
            for f in range(fields):
                third = n3[f] + tau * d2[f]
                mom_ref[f] = moments[f] + h * (
                    n1[f] + (h * 0.5) * (n2[f] + (h * (1.0 / 3.0)) * third)
                )
    for part in range(parts):
        advance(levels - 1, part)
    for copy in copies:
        copy.wait_send()


def per_device(
    sizes, state, coef, basis_quad, test_deriv, trace_vec, lift_vec, tent_height, elem_tent
):
    fields, basis, n_elem = state.shape
    levels, tent_dev = tent_height.shape
    pair = 2 * tent_dev
    wide = up(basis, LANES)
    crows = up(fields * fields + 1, 8)
    srows = up(levels * crows + levels, 8)
    chunk = min(256, n_elem)
    vmem = pl.BlockSpec(memory_space=pltpu.VMEM)
    return pl.pallas_call(
        functools.partial(kernel, sizes),
        out_shape=jax.ShapeDtypeStruct(state.shape, F32),
        in_specs=[vmem] * 8,
        out_specs=vmem,
        scratch_shapes=[
            pltpu.VMEM((levels, 3 * pair, n_elem), BF16),
            pltpu.VMEM((2 * wide, 2 * wide), BF16),
            pltpu.VMEM((crows, n_elem), F32),
            pltpu.VMEM((fields, ROWS, n_elem), F32),
            pltpu.VMEM((ROWS, n_elem), F32),
            pltpu.VMEM((levels, ROWS, n_elem), F32),
            pltpu.VMEM((fields, basis, chunk), F32),
            pltpu.VMEM((fields, 2 * wide, chunk), BF16),
            pltpu.VMEM((3, srows, pair), F32),
            pltpu.VMEM((4, srows, pair), F32),
            pltpu.VMEM((levels, 2, ROWS, pair), F32),
            pltpu.VMEM((levels, 4, ROWS, pair), F32),
            pltpu.VMEM((levels, ROWS, pair), F32),
            pltpu.VMEM((levels, 4, ROWS, pair), F32),
            pltpu.SemaphoreType.DMA((1 + 2 * levels, 4)),
            pltpu.SemaphoreType.DMA((1 + 2 * levels, 4)),
        ],
        compiler_params=pltpu.CompilerParams(
            collective_id=0, has_side_effects=True, vmem_limit_bytes=40 * 1024 * 1024
        ),
    )(
        state,
        coef,
        basis_quad,
        test_deriv,
        trace_vec.reshape(1, basis),
        lift_vec.reshape(1, basis),
        tent_height,
        elem_tent,
    )


def solution(mesh):
    split = ("gx", "gy")
    placed = (
        P(None, None, split),
        P(None, None, split),
        P(),
        P(),
        P(),
        P(),
        P(None, split),
        P(None, split),
    )
    sizes = (mesh.shape["gx"], mesh.shape["gy"])
    return jax.shard_map(
        functools.partial(per_device, sizes),
        mesh=mesh,
        in_specs=placed,
        out_specs=P(None, None, split),
        check_vma=False,
    )
```

```python
import functools

import jax
import jax.numpy as jnp
from jax import lax
from jax.experimental import pallas as pl
from jax.experimental.pallas import tpu as pltpu
from jax.sharding import PartitionSpec as P

F32 = jnp.float32
BF16 = jnp.bfloat16
MESH = pl.DeviceIdType.MESH
SCALE = 8.0
GROUP = 8
POWERS = 9
LANES = 128


def up(n, m):
    return -(-n // m) * m


NN = (((1,), (0,)), ((), ()))
NT = (((1,), (1,)), ((), ()))
TN = (((0,), (0,)), ((), ()))


def dot3(a, b, dims=NN):
    a_hi, a_lo = split2(a)
    b_hi, b_lo = split2(b)

    def one(x, y):
        return lax.dot_general(x, y, dims, preferred_element_type=F32)

    return one(a_hi, b_hi) + (one(a_hi, b_lo) + one(a_lo, b_hi))


def split2(x):
    hi = x.astype(BF16)
    lo = (x - hi.astype(F32)).astype(BF16)
    return hi, lo


def split3(x):
    hi = x.astype(BF16)
    rest = x - hi.astype(F32)
    mid = rest.astype(BF16)
    lo = (rest - mid.astype(F32)).astype(BF16)
    return jnp.concatenate([hi, mid, lo], axis=0)


def fold3(x):
    n = x.shape[0] // 3
    return x[:n] + (x[n : 2 * n] + x[2 * n :])


def seg_sum(x, onehot):
    return fold3(
        lax.dot_general(
            split3(x), onehot, (((1,), (1,)), ((), ())), preferred_element_type=F32
        )
    )


def seg_take(x, onehot):
    return fold3(jnp.dot(split3(x), onehot, preferred_element_type=F32))


def kernel(
    sizes,
    state_hbm,
    coef_hbm,
    bq_hbm,
    td_hbm,
    trace_hbm,
    lift_hbm,
    height_hbm,
    tent_hbm,
    out_ref,
    state_ref,
    coef_ref,
    bq_ref,
    td_ref,
    trace_ref,
    lift_ref,
    height_ref,
    tent_ref,
    hot_ref,
    lhs_ref,
    cs_ref,
    ct_ref,
    cube_ref,
    mom_ref,
    fin_ref,
    v1_ref,
    v2_ref,
    g_ref,
    stat_ref,
    stat_in,
    part_ref,
    part_in,
    tot_ref,
    tot_in,
    load_sem,
    send_sem,
    recv_sem,
):
    n_first, n_second = sizes
    fields, basis, n_elem = state_ref.shape
    levels, tent_dev = height_ref.shape
    pair = 2 * tent_dev
    wide = up(basis, LANES)
    crows = cs_ref.shape[0]
    me_first = lax.axis_index("gx")
    me_second = lax.axis_index("gy")
    next_first = lax.rem(me_first + 1, n_first)
    prev_first = lax.rem(me_first + n_first - 1, n_first)
    next_second = lax.rem(me_second + 1, n_second)
    prev_second = lax.rem(me_second + n_second - 1, n_second)
    peers = [
        (next_first, me_second),
        (prev_first, me_second),
        (me_first, next_second),
        (me_first, prev_second),
    ]

    barrier = pltpu.get_barrier_semaphore()
    for peer in peers:
        pl.semaphore_signal(barrier, inc=1, device_id=peer, device_id_type=MESH)
    loads = [
        pltpu.make_async_copy(src, dst, load_sem.at[i])
        for i, (src, dst) in enumerate(
            [
                (tent_hbm, tent_ref),
                (coef_hbm, coef_ref),
                (td_hbm, td_ref),
                (bq_hbm, bq_ref),
                (trace_hbm, trace_ref),
                (lift_hbm, lift_ref),
                (height_hbm, height_ref),
                (state_hbm, state_ref),
            ]
        )
    ]
    for load in loads:
        load.start()

    def remote(src, dst, slot, k):
        return pltpu.make_async_remote_copy(
            src_ref=src,
            dst_ref=dst,
            send_sem=send_sem.at[slot, k],
            recv_sem=recv_sem.at[slot, k],
            device_id=peers[k],
            device_id_type=MESH,
        )

    def build_hot(level):
        tents = tent_ref[level : level + 1, :]
        owner = tents // tent_dev
        local = tents - owner * tent_dev
        own_first = owner // n_second
        own_second = owner - own_first * n_second
        base = jnp.where(
            own_first == me_first,
            jnp.where(
                own_second == me_second,
                0,
                jnp.where(own_second == next_second, 2 * pair, 2 * pair + tent_dev),
            ),
            jnp.where(own_first == next_first, pair, pair + tent_dev),
        )
        column = base + local
        rows = lax.broadcasted_iota(jnp.int32, (3 * pair, n_elem), 0)
        hot_ref[level] = jnp.where(rows == column, 1.0, 0.0).astype(F32).astype(BF16)

    def send_stat(level):
        sums = seg_sum(cs_ref[...], hot_ref[level])
        for block in range(3):
            stat_ref[level, block, 0:crows, :] = sums[:, block * pair : (block + 1) * pair]
            stat_ref[level, block, crows:, :] = jnp.zeros(
                (stat_ref.shape[2] - crows, pair), F32
            )
            stat_ref[level, block, crows : crows + levels, 0:tent_dev] = (
                SCALE * height_ref[...]
            )
        if level == 0:
            pl.semaphore_wait(barrier, 4)
        copies = [
            remote(stat_ref.at[level, 1 + k // 2], stat_in.at[level, k], level, k)
            for k in range(4)
        ]
        for copy in copies:
            copy.start()
        return copies

    low = lax.broadcasted_iota(jnp.int32, (1, pair), 1) < tent_dev

    def table_of(own, arrived):
        return jnp.concatenate(
            [
                own,
                jnp.where(low, arrived[1], pltpu.roll(arrived[0], tent_dev, 1)),
                jnp.where(low, arrived[3], pltpu.roll(arrived[2], tent_dev, 1)),
            ],
            axis=1,
        )

    loads[0].wait()
    build_hot(0)
    loads[1].wait()
    cs_ref[...] = jnp.zeros_like(cs_ref)
    ct_ref[...] = jnp.zeros_like(ct_ref)
    for g in range(fields):
        cs_ref[g * fields : (g + 1) * fields, :] = coef_ref[g]
        for f in range(fields):
            ct_ref[f, g : g + 1, :] = coef_ref[g, f : f + 1, :]
    cs_ref[fields * fields : fields * fields + 1, :] = jnp.ones((1, n_elem), F32)
    for load in loads[2:7]:
        load.wait()
    stat_copies = [send_stat(0)]

    a = dot3(td_ref[...] * (1.0 / SCALE), bq_ref[...], TN)
    a2 = dot3(a, a)
    a3 = dot3(a2, a)
    lift_row = lift_ref[...] * (1.0 / SCALE)
    r0 = trace_ref[...]
    r1 = dot3(r0, a)
    r2 = dot3(r0, a2)
    r02 = jnp.concatenate([r0, r1, r2], axis=0)
    r35 = dot3(r02, a3)
    r68 = dot3(r35, a3)
    powers = jnp.concatenate(
        [r02, r35, r68, jnp.zeros((16 - POWERS, basis), F32)], axis=0
    )
    taus = jnp.sum(powers * lift_row, axis=1, keepdims=True)
    tau = [taus[j : j + 1] for j in range(POWERS)]

    p_hi, p_lo = split2(powers)
    p_all = jnp.concatenate([p_hi, p_lo], axis=0)
    loads[7].wait()
    mom_ref[...] = jnp.zeros_like(mom_ref)
    for f in range(fields):
        s_hi, s_lo = split2(state_ref[f])
        both = jnp.dot(p_all, s_hi, preferred_element_type=F32)
        rest = jnp.dot(p_hi, s_lo, preferred_element_type=F32)
        found = both[:16] + (both[16:] + rest)
        for j in range(POWERS):
            mom_ref[j, f : f + 1, :] = found[j : j + 1]

    def times(v):
        total = ct_ref[0] * v[0:1]
        for f in range(1, fields):
            total = total + ct_ref[f] * v[f : f + 1]
        return total

    def operator(slot, matrix):
        pad = jnp.concatenate([matrix, jnp.zeros((wide - basis, basis), F32)], axis=0)
        lhs_ref[slot] = jnp.zeros((2 * wide, 2 * wide), BF16)
        hi, lo = split2(pad)
        for at in (0, wide):
            lhs_ref[slot, 0:wide, at : at + basis] = hi
            lhs_ref[slot, wide:, at : at + basis] = lo

    def apply(slot, matrices, source, target, terms, bases):
        step = min(2 * LANES, n_elem)
        zeros = jnp.zeros((wide - basis, LANES), F32)
        for start in range(0, n_elem, step):
            for lane in range(start, start + step, LANES):
                at = slice(lane, lane + LANES)
                bc = [
                    [
                        jnp.broadcast_to(matrices(g, f, at), (16, LANES))
                        for f in range(fields)
                    ]
                    for g in range(fields)
                ]
                for row in range(0, wide, 16):
                    size = min(16, basis - row)
                    v = [source[f, row : row + size, at] for f in range(fields)]
                    for g in range(fields):
                        total = bc[g][0][:size] * v[0]
                        for f in range(1, fields):
                            total = total + bc[g][f][:size] * v[f]
                        if size < 16:
                            total = jnp.concatenate([total, zeros], axis=0)
                        hi, lo = split2(total)
                        g_ref[g, row : row + 16, at] = hi
                        g_ref[g, wide + row : wide + row + 16, at] = lo
            lanes = slice(start, start + step)
            for g in range(fields):
                res = jnp.dot(
                    lhs_ref[slot], g_ref[g, :, lanes], preferred_element_type=F32
                )
                total = res[:basis] + res[wide : wide + basis]
                for term, base in zip(terms, bases):
                    value = base[g, :, lanes]
                    total = total + (value if term is None else term[:, lanes] * value)
                target[g, :, lanes] = total

    def own_matrix(g, f, at):
        return coef_ref[g, f : f + 1, at]

    def scaled_cube(g, f, at):
        return cube_ref[1, g, f : f + 1, at]

    def cube(g, f, at):
        return cube_ref[0, g, f : f + 1, at]

    moments = [mom_ref[j] for j in range(POWERS)]
    lifted = []
    copies = []
    poly = []
    heights = []
    for level in range(levels):
        count = len(moments)
        p1 = [times(moments[j + 1]) for j in range(count - 1)]
        sent = jnp.concatenate(
            [moments[0], p1[0], times(p1[1] - tau[1] * moments[0])], axis=0
        )
        sums = seg_sum(sent, hot_ref[level])
        for block in range(2):
            part_ref[level, block] = sums[:, (1 + block) * pair : (2 + block) * pair]
        going = [
            remote(part_ref.at[level, k // 2], part_in.at[level, k], levels + level, k)
            for k in range(4)
        ]
        for copy in going:
            copy.start()

        p2 = [times(p1[j + 1]) for j in range(count - 2)]
        p3 = [times(p2[j + 1]) for j in range(count - 3)]
        if level == 0:
            for later in range(1, levels):
                build_hot(later)
                stat_copies.append(send_stat(later))
            operator(0, a)
            operator(1, a3)
        elif level == 1:
            apply(0, own_matrix, v1_ref, v2_ref, [], [])
        else:
            z = [poly[6], poly[7], poly[8]]
            apply(1, scaled_cube, state_ref, out_ref, z, [state_ref, v1_ref, v2_ref])
            z = [poly[3], poly[4], poly[5]]
            apply(1, cube, out_ref, out_ref, z, [state_ref, v1_ref, v2_ref])

        for copy in stat_copies[level]:
            copy.wait_recv()
        for copy in going:
            copy.wait_recv()
        own = sums[:, :pair] + part_in[level, 0] + part_in[level, 2]
        own = own + pltpu.roll(part_in[level, 1] + part_in[level, 3], tent_dev, 1)
        stat = stat_ref[level, 0] + stat_in[level, 0] + stat_in[level, 2]
        stat = stat + pltpu.roll(stat_in[level, 1] + stat_in[level, 3], tent_dev, 1)
        per = 1.0 / jnp.maximum(stat[fields * fields : fields * fields + 1], 1.0)
        tot_ref[level, 0 : 2 * GROUP, :] = own[: 2 * GROUP] * per
        tot_ref[level, 2 * GROUP :, :] = jnp.zeros((GROUP, pair), F32)
        for g in range(fields):
            joint = stat[g * fields : g * fields + 1] * (own[0:1] * per)
            for f in range(1, fields):
                joint = joint + stat[g * fields + f : g * fields + f + 1] * (
                    own[f : f + 1] * per
                )
            row = 2 * GROUP + g
            tot_ref[level, row : row + 1, :] = (
                own[row : row + 1] + tau[1] * joint
            ) * per
        back = [
            remote(tot_ref.at[level], tot_in.at[level, k], 2 * levels + level, k)
            for k in range(4)
        ]
        for copy in back:
            copy.start()
        copies += going + back

        if level == 0:
            arrived = [stat_in[0, k, crows:, :] for k in range(4)]
            table = table_of(stat_ref[0, 0, crows:, :], arrived)
            for later in range(levels):
                found = seg_take(table, hot_ref[later])
                heights.append(found[later : later + 1])
            poly = [None]
            for h in heights:
                by = [h, h * h * 0.5, h * h * h * (1.0 / 6.0)]
                longer = list(poly) + [0.0] * 3
                for i, value in enumerate(poly):
                    for k in range(3):
                        term = by[k] if value is None else value * by[k]
                        longer[i + k + 1] = longer[i + k + 1] + term
                poly = longer
            apply(0, own_matrix, state_ref, v1_ref, [], [])
        elif level == 1:
            for g in range(fields):
                row = coef_ref[g]
                for _ in range(2):
                    total = row[0:1] * coef_ref[0]
                    for f in range(1, fields):
                        total = total + row[f : f + 1] * coef_ref[f]
                    row = total
                cube_ref[0, g] = row
                cube_ref[1, g] = row * poly[9]
        else:
            z = [None, poly[1], poly[2]]
            apply(1, cube, out_ref, out_ref, z, [state_ref, v1_ref, v2_ref])
        h = heights[level]
        h2 = h * h * 0.5
        h3 = h * h * h * (1.0 / 6.0)
        still = [
            moments[j] + h * p1[j] + h2 * p2[j] + h3 * p3[j] for j in range(count - 3)
        ]
        grown = list(lifted) + [0.0] * 3
        power = list(lifted)
        for k, weight in enumerate([h, h2, h3]):
            power = [times(v) for v in power]
            for j, v in enumerate(power):
                grown[j + k + 1] = grown[j + k + 1] + weight * v
        if level == levels - 1:
            l0 = lift_row
            l1 = dot3(l0, a, NT)
            l2 = dot3(l0, a2, NT)
            l02 = jnp.concatenate([l0, l1, l2], axis=0)
            l35 = dot3(l02, a3, NT)
            l68 = dot3(l35, a3, NT)
            ladder = jnp.concatenate(
                [l02, l35, l68, jnp.zeros((16 - POWERS, basis), F32)], axis=0
            )
            ladder = jnp.concatenate(
                [ladder, jnp.zeros((16, wide - basis), F32)], axis=1
            )
            l_hi, l_lo = split2(ladder)
            l_hi = l_hi.astype(F32)
            ladder = jnp.concatenate(
                [l_hi, l_hi, l_lo.astype(F32), jnp.zeros((wide - 48, wide), F32)],
                axis=0,
            ).T.astype(BF16)
            fin_ref[...] = jnp.zeros_like(fin_ref)

        for copy in back:
            copy.wait_recv()
        each = seg_take(
            table_of(tot_ref[level], [tot_in[level, k] for k in range(4)]),
            hot_ref[level],
        )
        d0 = each[:GROUP] - moments[0]
        d1 = each[GROUP : 2 * GROUP] - (p1[0] + tau[0] * d0)
        cd0 = times(d0)
        d2 = each[2 * GROUP :] - (p2[0] + tau[1] * cd0 + tau[0] * d1)
        q = [
            h * d0 + h2 * d1 + h3 * d2,
            h2 * cd0 + h3 * times(d1),
            h3 * times(cd0),
        ]
        moments = [
            still[j] + tau[j] * q[0] + tau[j + 1] * q[1] + tau[j + 2] * q[2]
            for j in range(count - 3)
        ]
        for j in range(3):
            grown[j] = grown[j] + q[j]
        lifted = grown

    for j in range(POWERS):
        for f in range(fields):
            fin_ref[f, j : j + 1, :] = lifted[j][f : f + 1]
    for f in range(fields):
        c_hi, c_lo = split2(fin_ref[f])
        rhs = jnp.concatenate([c_hi, c_lo, c_hi], axis=0)
        res = jnp.dot(ladder[:, :48], rhs, preferred_element_type=F32)
        out_ref[f] = out_ref[f] + res[:basis]
    for group in stat_copies:
        for copy in group:
            copy.wait_send()
    for copy in copies:
        copy.wait_send()


def per_device(
    sizes, state, coef, basis_quad, test_deriv, trace_vec, lift_vec, tent_height, elem_tent
):
    fields, basis, n_elem = state.shape
    levels, tent_dev = tent_height.shape
    pair = 2 * tent_dev
    wide = up(basis, LANES)
    crows = up(fields * fields + 1, 8)
    srows = crows + up(levels, 8)
    vmem = pl.BlockSpec(memory_space=pltpu.VMEM)
    hbm = pl.BlockSpec(memory_space=pltpu.HBM)
    operands = (
        state,
        coef,
        basis_quad,
        test_deriv.T,
        trace_vec.reshape(1, basis),
        lift_vec.reshape(1, basis),
        tent_height,
        elem_tent,
    )
    return pl.pallas_call(
        functools.partial(kernel, sizes),
        out_shape=jax.ShapeDtypeStruct(state.shape, F32),
        in_specs=[hbm] * 8,
        out_specs=vmem,
        scratch_shapes=[pltpu.VMEM(x.shape, x.dtype) for x in operands]
        + [
            pltpu.VMEM((levels, 3 * pair, n_elem), BF16),
            pltpu.VMEM((2, 2 * wide, 2 * wide), BF16),
            pltpu.VMEM((crows, n_elem), F32),
            pltpu.VMEM((fields, GROUP, n_elem), F32),
            pltpu.VMEM((2, fields, fields, n_elem), F32),
            pltpu.VMEM((POWERS, GROUP, n_elem), F32),
            pltpu.VMEM((fields, 16, n_elem), F32),
            pltpu.VMEM(state.shape, F32),
            pltpu.VMEM(state.shape, F32),
            pltpu.VMEM((fields, 2 * wide, n_elem), BF16),
            pltpu.VMEM((levels, 3, srows, pair), F32),
            pltpu.VMEM((levels, 4, srows, pair), F32),
            pltpu.VMEM((levels, 2, 3 * GROUP, pair), F32),
            pltpu.VMEM((levels, 4, 3 * GROUP, pair), F32),
            pltpu.VMEM((levels, 3 * GROUP, pair), F32),
            pltpu.VMEM((levels, 4, 3 * GROUP, pair), F32),
            pltpu.SemaphoreType.DMA((8,)),
            pltpu.SemaphoreType.DMA((3 * levels, 4)),
            pltpu.SemaphoreType.DMA((3 * levels, 4)),
        ],
        compiler_params=pltpu.CompilerParams(
            collective_id=0, has_side_effects=True, vmem_limit_bytes=63 * 1024 * 1024
        ),
    )(*operands)


def solution(mesh):
    split = ("gx", "gy")
    placed = (
        P(None, None, split),
        P(None, None, split),
        P(),
        P(),
        P(),
        P(),
        P(None, split),
        P(None, split),
    )
    sizes = (mesh.shape["gx"], mesh.shape["gy"])
    return jax.shard_map(
        functools.partial(per_device, sizes),
        mesh=mesh,
        in_specs=placed,
        out_specs=P(None, None, split),
        check_vma=False,
    )
```

```python
import functools

import jax
import jax.numpy as jnp
from jax import lax
from jax.experimental import pallas as pl
from jax.experimental.pallas import tpu as pltpu
from jax.sharding import PartitionSpec as P

F32 = jnp.float32
BF16 = jnp.bfloat16
MESH = pl.DeviceIdType.MESH
SCALE = 8.0
GROUP = 8
POWERS = 9
LANES = 128


def up(n, m):
    return -(-n // m) * m


NN = (((1,), (0,)), ((), ()))
NT = (((1,), (1,)), ((), ()))
TN = (((0,), (0,)), ((), ()))


def dot3(a, b, dims=NN):
    a_hi, a_lo = split2(a)
    b_hi, b_lo = split2(b)

    def one(x, y):
        return lax.dot_general(x, y, dims, preferred_element_type=F32)

    return one(a_hi, b_hi) + (one(a_hi, b_lo) + one(a_lo, b_hi))


def split2(x):
    hi = x.astype(BF16)
    lo = (x - hi.astype(F32)).astype(BF16)
    return hi, lo


def split3(x):
    hi = x.astype(BF16)
    rest = x - hi.astype(F32)
    mid = rest.astype(BF16)
    lo = (rest - mid.astype(F32)).astype(BF16)
    return jnp.concatenate([hi, mid, lo], axis=0)


def fold3(x):
    n = x.shape[0] // 3
    return x[:n] + (x[n : 2 * n] + x[2 * n :])


def seg_sum(x, onehot):
    return fold3(
        lax.dot_general(
            split3(x), onehot, (((1,), (1,)), ((), ())), preferred_element_type=F32
        )
    )


def seg_take(x, onehot):
    return fold3(jnp.dot(split3(x), onehot, preferred_element_type=F32))


def kernel(
    sizes,
    state_hbm,
    coef_hbm,
    bq_hbm,
    td_hbm,
    trace_hbm,
    lift_hbm,
    height_hbm,
    tent_hbm,
    still_hbm,
    fin_ref,
    ladder_ref,
    out_ref,
    state_ref,
    coef_ref,
    bq_ref,
    td_ref,
    trace_ref,
    lift_ref,
    height_ref,
    tent_ref,
    hot_ref,
    lhs_ref,
    cs_ref,
    ct_ref,
    cube_ref,
    mom_ref,
    v1_ref,
    v2_ref,
    g_ref,
    stat_ref,
    stat_in,
    part_ref,
    part_in,
    tot_ref,
    tot_in,
    load_sem,
    save_sem,
    send_sem,
    recv_sem,
):
    n_first, n_second = sizes
    fields, basis, n_elem = state_ref.shape
    levels, tent_dev = height_ref.shape
    pair = 2 * tent_dev
    wide = up(basis, LANES)
    crows = cs_ref.shape[0]
    me_first = lax.axis_index("gx")
    me_second = lax.axis_index("gy")
    next_first = lax.rem(me_first + 1, n_first)
    prev_first = lax.rem(me_first + n_first - 1, n_first)
    next_second = lax.rem(me_second + 1, n_second)
    prev_second = lax.rem(me_second + n_second - 1, n_second)
    peers = [
        (next_first, me_second),
        (prev_first, me_second),
        (me_first, next_second),
        (me_first, prev_second),
    ]

    barrier = pltpu.get_barrier_semaphore()
    for peer in peers:
        pl.semaphore_signal(barrier, inc=1, device_id=peer, device_id_type=MESH)
    loads = [
        pltpu.make_async_copy(src, dst, load_sem.at[i])
        for i, (src, dst) in enumerate(
            [
                (tent_hbm, tent_ref),
                (coef_hbm, coef_ref),
                (td_hbm, td_ref),
                (bq_hbm, bq_ref),
                (trace_hbm, trace_ref),
                (lift_hbm, lift_ref),
                (height_hbm, height_ref),
                (state_hbm, state_ref),
            ]
        )
    ]
    for load in loads:
        load.start()

    def remote(src, dst, slot, k):
        return pltpu.make_async_remote_copy(
            src_ref=src,
            dst_ref=dst,
            send_sem=send_sem.at[slot, k],
            recv_sem=recv_sem.at[slot, k],
            device_id=peers[k],
            device_id_type=MESH,
        )

    def build_hot(level):
        tents = tent_ref[level : level + 1, :]
        owner = tents // tent_dev
        local = tents - owner * tent_dev
        own_first = owner // n_second
        own_second = owner - own_first * n_second
        base = jnp.where(
            own_first == me_first,
            jnp.where(
                own_second == me_second,
                0,
                jnp.where(own_second == next_second, 2 * pair, 2 * pair + tent_dev),
            ),
            jnp.where(own_first == next_first, pair, pair + tent_dev),
        )
        column = base + local
        rows = lax.broadcasted_iota(jnp.int32, (3 * pair, n_elem), 0)
        hot_ref[level] = jnp.where(rows == column, 1.0, 0.0).astype(F32).astype(BF16)

    def send_stat(level):
        sums = seg_sum(cs_ref[...], hot_ref[level])
        for block in range(3):
            stat_ref[level, block, 0:crows, :] = sums[:, block * pair : (block + 1) * pair]
            stat_ref[level, block, crows:, :] = jnp.zeros(
                (stat_ref.shape[2] - crows, pair), F32
            )
            stat_ref[level, block, crows : crows + levels, 0:tent_dev] = (
                SCALE * height_ref[...]
            )
        if level == 0:
            pl.semaphore_wait(barrier, 4)
        copies = [
            remote(stat_ref.at[level, 1 + k // 2], stat_in.at[level, k], level, k)
            for k in range(4)
        ]
        for copy in copies:
            copy.start()
        return copies

    low = lax.broadcasted_iota(jnp.int32, (1, pair), 1) < tent_dev

    def table_of(own, arrived):
        return jnp.concatenate(
            [
                own,
                jnp.where(low, arrived[1], pltpu.roll(arrived[0], tent_dev, 1)),
                jnp.where(low, arrived[3], pltpu.roll(arrived[2], tent_dev, 1)),
            ],
            axis=1,
        )

    loads[0].wait()
    build_hot(0)
    loads[1].wait()
    cs_ref[...] = jnp.zeros_like(cs_ref)
    ct_ref[...] = jnp.zeros_like(ct_ref)
    for g in range(fields):
        cs_ref[g * fields : (g + 1) * fields, :] = coef_ref[g]
        for f in range(fields):
            ct_ref[f, g : g + 1, :] = coef_ref[g, f : f + 1, :]
    cs_ref[fields * fields : fields * fields + 1, :] = jnp.ones((1, n_elem), F32)
    for load in loads[2:7]:
        load.wait()
    stat_copies = [send_stat(0)]

    a = dot3(td_ref[...] * (1.0 / SCALE), bq_ref[...], TN)
    a2 = dot3(a, a)
    a3 = dot3(a2, a)
    lift_row = lift_ref[...] * (1.0 / SCALE)
    r0 = trace_ref[...]
    r1 = dot3(r0, a)
    r2 = dot3(r0, a2)
    r02 = jnp.concatenate([r0, r1, r2], axis=0)
    r35 = dot3(r02, a3)
    r68 = dot3(r35, a3)
    powers = jnp.concatenate(
        [r02, r35, r68, jnp.zeros((16 - POWERS, basis), F32)], axis=0
    )
    taus = jnp.sum(powers * lift_row, axis=1, keepdims=True)
    tau = [taus[j : j + 1] for j in range(POWERS)]

    p_hi, p_lo = split2(powers)
    p_all = jnp.concatenate([p_hi, p_lo], axis=0)
    loads[7].wait()
    mom_ref[...] = jnp.zeros_like(mom_ref)
    for f in range(fields):
        s_hi, s_lo = split2(state_ref[f])
        both = jnp.dot(p_all, s_hi, preferred_element_type=F32)
        rest = jnp.dot(p_hi, s_lo, preferred_element_type=F32)
        found = both[:16] + (both[16:] + rest)
        for j in range(POWERS):
            mom_ref[j, f : f + 1, :] = found[j : j + 1]

    def times(v):
        total = ct_ref[0] * v[0:1]
        for f in range(1, fields):
            total = total + ct_ref[f] * v[f : f + 1]
        return total

    def operator(slot, matrix):
        pad = jnp.concatenate([matrix, jnp.zeros((wide - basis, basis), F32)], axis=0)
        lhs_ref[slot] = jnp.zeros((2 * wide, 2 * wide), BF16)
        hi, lo = split2(pad)
        for at in (0, wide):
            lhs_ref[slot, 0:wide, at : at + basis] = hi
            lhs_ref[slot, wide:, at : at + basis] = lo

    def apply(slot, matrices, source, target, terms, bases):
        step = min(2 * LANES, n_elem)
        zeros = jnp.zeros((wide - basis, LANES), F32)
        for start in range(0, n_elem, step):
            for lane in range(start, start + step, LANES):
                at = slice(lane, lane + LANES)
                bc = [
                    [
                        jnp.broadcast_to(matrices(g, f, at), (16, LANES))
                        for f in range(fields)
                    ]
                    for g in range(fields)
                ]
                for row in range(0, wide, 16):
                    size = min(16, basis - row)
                    v = [source[f, row : row + size, at] for f in range(fields)]
                    for g in range(fields):
                        total = bc[g][0][:size] * v[0]
                        for f in range(1, fields):
                            total = total + bc[g][f][:size] * v[f]
                        if size < 16:
                            total = jnp.concatenate([total, zeros], axis=0)
                        hi, lo = split2(total)
                        g_ref[g, row : row + 16, at] = hi
                        g_ref[g, wide + row : wide + row + 16, at] = lo
            lanes = slice(start, start + step)
            for g in range(fields):
                res = jnp.dot(
                    lhs_ref[slot], g_ref[g, :, lanes], preferred_element_type=F32
                )
                total = res[:basis] + res[wide : wide + basis]
                for term, base in zip(terms, bases):
                    value = base[g, :, lanes]
                    total = total + (value if term is None else term[:, lanes] * value)
                target[g, :, lanes] = total

    def own_matrix(g, f, at):
        return coef_ref[g, f : f + 1, at]

    def scaled_cube(g, f, at):
        return cube_ref[1, g, f : f + 1, at]

    def cube(g, f, at):
        return cube_ref[0, g, f : f + 1, at]

    moments = [mom_ref[j] for j in range(POWERS)]
    lifted = []
    copies = []
    poly = []
    heights = []
    for level in range(levels):
        count = len(moments)
        p1 = [times(moments[j + 1]) for j in range(count - 1)]
        sent = jnp.concatenate(
            [moments[0], p1[0], times(p1[1] - tau[1] * moments[0])], axis=0
        )
        sums = seg_sum(sent, hot_ref[level])
        for block in range(2):
            part_ref[level, block] = sums[:, (1 + block) * pair : (2 + block) * pair]
        going = [
            remote(part_ref.at[level, k // 2], part_in.at[level, k], levels + level, k)
            for k in range(4)
        ]
        for copy in going:
            copy.start()

        p2 = [times(p1[j + 1]) for j in range(count - 2)]
        p3 = [times(p2[j + 1]) for j in range(count - 3)]
        if level == 0:
            for later in range(1, levels):
                build_hot(later)
                stat_copies.append(send_stat(later))
            operator(0, a)
            operator(1, a3)
        elif level == 1:
            apply(0, own_matrix, v1_ref, v2_ref, [], [])
        else:
            z = [poly[3], poly[4], poly[5]]
            apply(1, cube, out_ref, out_ref, z, [state_ref, v1_ref, v2_ref])

        for copy in stat_copies[level]:
            copy.wait_recv()
        for copy in going:
            copy.wait_recv()
        own = sums[:, :pair] + part_in[level, 0] + part_in[level, 2]
        own = own + pltpu.roll(part_in[level, 1] + part_in[level, 3], tent_dev, 1)
        stat = stat_ref[level, 0] + stat_in[level, 0] + stat_in[level, 2]
        stat = stat + pltpu.roll(stat_in[level, 1] + stat_in[level, 3], tent_dev, 1)
        per = 1.0 / jnp.maximum(stat[fields * fields : fields * fields + 1], 1.0)
        tot_ref[level, 0 : 2 * GROUP, :] = own[: 2 * GROUP] * per
        tot_ref[level, 2 * GROUP :, :] = jnp.zeros((GROUP, pair), F32)
        for g in range(fields):
            joint = stat[g * fields : g * fields + 1] * (own[0:1] * per)
            for f in range(1, fields):
                joint = joint + stat[g * fields + f : g * fields + f + 1] * (
                    own[f : f + 1] * per
                )
            row = 2 * GROUP + g
            tot_ref[level, row : row + 1, :] = (
                own[row : row + 1] + tau[1] * joint
            ) * per
        back = [
            remote(tot_ref.at[level], tot_in.at[level, k], 2 * levels + level, k)
            for k in range(4)
        ]
        for copy in back:
            copy.start()
        copies += going + back

        if level == 0:
            arrived = [stat_in[0, k, crows:, :] for k in range(4)]
            table = table_of(stat_ref[0, 0, crows:, :], arrived)
            for later in range(levels):
                found = seg_take(table, hot_ref[later])
                heights.append(found[later : later + 1])
            poly = [None]
            for h in heights:
                by = [h, h * h * 0.5, h * h * h * (1.0 / 6.0)]
                longer = list(poly) + [0.0] * 3
                for i, value in enumerate(poly):
                    for k in range(3):
                        term = by[k] if value is None else value * by[k]
                        longer[i + k + 1] = longer[i + k + 1] + term
                poly = longer
            apply(0, own_matrix, state_ref, v1_ref, [], [])
        elif level == 1:
            for g in range(fields):
                row = coef_ref[g]
                for _ in range(2):
                    total = row[0:1] * coef_ref[0]
                    for f in range(1, fields):
                        total = total + row[f : f + 1] * coef_ref[f]
                    row = total
                cube_ref[0, g] = row
                cube_ref[1, g] = row * poly[9]
            z = [poly[6], poly[7], poly[8]]
            apply(1, scaled_cube, state_ref, out_ref, z, [state_ref, v1_ref, v2_ref])
        else:
            z = [None, poly[1], poly[2]]
            apply(1, cube, out_ref, out_ref, z, [state_ref, v1_ref, v2_ref])
            save = pltpu.make_async_copy(out_ref, still_hbm, save_sem.at[0])
            save.start()
        h = heights[level]
        h2 = h * h * 0.5
        h3 = h * h * h * (1.0 / 6.0)
        still = [
            moments[j] + h * p1[j] + h2 * p2[j] + h3 * p3[j] for j in range(count - 3)
        ]
        grown = list(lifted) + [0.0] * 3
        power = list(lifted)
        for k, weight in enumerate([h, h2, h3]):
            power = [times(v) for v in power]
            for j, v in enumerate(power):
                grown[j + k + 1] = grown[j + k + 1] + weight * v
        if level == levels - 1:
            l0 = lift_row
            l1 = dot3(l0, a, NT)
            l2 = dot3(l0, a2, NT)
            l02 = jnp.concatenate([l0, l1, l2], axis=0)
            l35 = dot3(l02, a3, NT)
            l68 = dot3(l35, a3, NT)
            ladder = jnp.concatenate(
                [l02, l35, l68, jnp.zeros((16 - POWERS, basis), F32)], axis=0
            )
            ladder = jnp.concatenate(
                [ladder, jnp.zeros((16, wide - basis), F32)], axis=1
            )
            l_hi, l_lo = split2(ladder)
            l_hi = l_hi.astype(F32)
            ladder_ref[...] = jnp.concatenate(
                [l_hi, l_hi, l_lo.astype(F32), jnp.zeros((wide - 48, wide), F32)],
                axis=0,
            ).T.astype(BF16)
            fin_ref[...] = jnp.zeros_like(fin_ref)

        for copy in back:
            copy.wait_recv()
        each = seg_take(
            table_of(tot_ref[level], [tot_in[level, k] for k in range(4)]),
            hot_ref[level],
        )
        d0 = each[:GROUP] - moments[0]
        d1 = each[GROUP : 2 * GROUP] - (p1[0] + tau[0] * d0)
        cd0 = times(d0)
        d2 = each[2 * GROUP :] - (p2[0] + tau[1] * cd0 + tau[0] * d1)
        q = [
            h * d0 + h2 * d1 + h3 * d2,
            h2 * cd0 + h3 * times(d1),
            h3 * times(cd0),
        ]
        moments = [
            still[j] + tau[j] * q[0] + tau[j + 1] * q[1] + tau[j + 2] * q[2]
            for j in range(count - 3)
        ]
        for j in range(3):
            grown[j] = grown[j] + q[j]
        lifted = grown

    for j in range(POWERS):
        for f in range(fields):
            fin_ref[f, j : j + 1, :] = lifted[j][f : f + 1]
    save.wait()
    for group in stat_copies:
        for copy in group:
            copy.wait_send()
    for copy in copies:
        copy.wait_send()


def add_fluxes(still_ref, fin_ref, ladder_ref, out_ref):
    c_hi, c_lo = split2(fin_ref[0])
    rhs = jnp.concatenate([c_hi, c_lo, c_hi], axis=0)
    res = jnp.dot(ladder_ref[:, :48], rhs, preferred_element_type=F32)
    out_ref[0] = still_ref[0] + res[: out_ref.shape[1]]


def per_device(
    sizes, state, coef, basis_quad, test_deriv, trace_vec, lift_vec, tent_height, elem_tent
):
    fields, basis, n_elem = state.shape
    levels, tent_dev = tent_height.shape
    pair = 2 * tent_dev
    wide = up(basis, LANES)
    crows = up(fields * fields + 1, 8)
    srows = crows + up(levels, 8)
    vmem = pl.BlockSpec(memory_space=pltpu.VMEM)
    hbm = pl.BlockSpec(memory_space=pltpu.HBM)
    operands = (
        state,
        coef,
        basis_quad,
        test_deriv.T,
        trace_vec.reshape(1, basis),
        lift_vec.reshape(1, basis),
        tent_height,
        elem_tent,
    )
    still, fluxes, ladder = pl.pallas_call(
        functools.partial(kernel, sizes),
        out_shape=[
            jax.ShapeDtypeStruct(state.shape, F32),
            jax.ShapeDtypeStruct((fields, 16, n_elem), F32),
            jax.ShapeDtypeStruct((wide, wide), BF16),
        ],
        in_specs=[hbm] * 8,
        out_specs=[hbm, vmem, vmem],
        scratch_shapes=[pltpu.VMEM(state.shape, F32)]
        + [pltpu.VMEM(x.shape, x.dtype) for x in operands]
        + [
            pltpu.VMEM((levels, 3 * pair, n_elem), BF16),
            pltpu.VMEM((2, 2 * wide, 2 * wide), BF16),
            pltpu.VMEM((crows, n_elem), F32),
            pltpu.VMEM((fields, GROUP, n_elem), F32),
            pltpu.VMEM((2, fields, fields, n_elem), F32),
            pltpu.VMEM((POWERS, GROUP, n_elem), F32),
            pltpu.VMEM(state.shape, F32),
            pltpu.VMEM(state.shape, F32),
            pltpu.VMEM((fields, 2 * wide, n_elem), BF16),
            pltpu.VMEM((levels, 3, srows, pair), F32),
            pltpu.VMEM((levels, 4, srows, pair), F32),
            pltpu.VMEM((levels, 2, 3 * GROUP, pair), F32),
            pltpu.VMEM((levels, 4, 3 * GROUP, pair), F32),
            pltpu.VMEM((levels, 3 * GROUP, pair), F32),
            pltpu.VMEM((levels, 4, 3 * GROUP, pair), F32),
            pltpu.SemaphoreType.DMA((8,)),
            pltpu.SemaphoreType.DMA((1,)),
            pltpu.SemaphoreType.DMA((3 * levels, 4)),
            pltpu.SemaphoreType.DMA((3 * levels, 4)),
        ],
        compiler_params=pltpu.CompilerParams(
            collective_id=0, has_side_effects=True, vmem_limit_bytes=63 * 1024 * 1024
        ),
    )(*operands)
    return pl.pallas_call(
        add_fluxes,
        grid=(fields,),
        out_shape=jax.ShapeDtypeStruct(state.shape, F32),
        in_specs=[
            pl.BlockSpec((1, basis, n_elem), lambda f: (f, 0, 0)),
            pl.BlockSpec((1, 16, n_elem), lambda f: (f, 0, 0)),
            pl.BlockSpec((wide, wide), lambda f: (0, 0)),
        ],
        out_specs=pl.BlockSpec((1, basis, n_elem), lambda f: (f, 0, 0)),
        compiler_params=pltpu.CompilerParams(vmem_limit_bytes=63 * 1024 * 1024),
    )(still, fluxes, ladder)


def solution(mesh):
    split = ("gx", "gy")
    placed = (
        P(None, None, split),
        P(None, None, split),
        P(),
        P(),
        P(),
        P(),
        P(None, split),
        P(None, split),
    )
    sizes = (mesh.shape["gx"], mesh.shape["gy"])
    return jax.shard_map(
        functools.partial(per_device, sizes),
        mesh=mesh,
        in_specs=placed,
        out_specs=P(None, None, split),
        check_vma=False,
    )
```
